256 devices in a mesh: ctx: 64 (over z, y, core), tp: 4 (over x).
Axes of the slice: x: 4, y: 4, z: 8, core: 2. Of those that a mesh axis runs over, the one named last changes fastest.
Arguments:
- queries: bfloat16 [8192, 4096], P('ctx', 'tp'), may hold values from -7 to 7
- out_grad: bfloat16 [8192, 4096], P('ctx', 'tp'), may hold values from -6 to 6
- image_kv: bfloat16 [64, 2, 6404, 512], P('ctx', None, None, 'tp'), may hold values from -6 to 6
- tiles: int32 [64], replicated, may hold values from 1 to 4, as said below
- span_start: int32 [64], replicated, may hold values from 0 to 8191, as said below
- span_end: int32 [64], replicated, may hold values from 1 to 8192, as said below
- image_owner: int32 [64], replicated, may hold values from 0 to 63, as said below
Outputs:
- grad_queries: bfloat16 [8192, 4096], P('ctx', 'tp')
- grad_image_kv: bfloat16 [64, 2, 6404, 512], P('ctx', None, None, 'tp')
The draws below stay inside these ranges and needn't reach their ends.
Inputs may be any that keep to these rules, and one draw needn't show every extreme that they name: image_owner[s] is s or s - 1 (0 for s = 0): a span attends its own slot or the one before. s * 128 <= span_start[s] < s * 128 + 128 // 4. s * 128 + 3 * 32 < span_end[s] <= (s + 1) * 128. Some slot holds 4 tiles.
All inputs are finite; a program needn't handle non-finite values.
Results may differ from the reference program's by a relative error of at most 0.01.
Values may be sent and summed in bfloat16 or wider, within the bound.
No kernel may reach another device: no remote copies, remote signals or barrier semaphores. Data moves between devices by JAX's collectives and lax.ppermute only.
A program may use at most 192 MiB of HBM per device.

```python
import jax
import jax.numpy as jnp
from jax import lax

HEADS = 32
KV_HEADS = 4
HEAD = 128
TILE_ROWS = 1601
MAX_TILES = 4
TOK_DEV = 128
TOKENS = 8192
IMAGES = 64
SPANS = 64
ROWS_IMG = 6404


def draw_queries(key, part):
    key = jax.random.fold_in(key, 11)
    values = jnp.clip(jax.random.normal(key, (TOKENS, HEADS * HEAD), jnp.float32), -6.0, 6.0)
    return values.astype(jnp.bfloat16)


def draw_image_kv(key, part):
    key = jax.random.fold_in(key, 12)
    shape = (IMAGES, 2, ROWS_IMG, KV_HEADS * HEAD)
    values = jnp.clip(jax.random.normal(key, shape, jnp.float32), -6.0, 6.0)
    return values.astype(jnp.bfloat16)


def draw_tiles(key, part):
    key = jax.random.fold_in(key, 13)
    first, second = jax.random.split(key)
    counts = jax.random.randint(first, (IMAGES,), 1, MAX_TILES + 1)
    fullest = jax.random.randint(second, (), 0, IMAGES)
    return jnp.where(jnp.arange(IMAGES) == fullest, MAX_TILES, counts).astype(jnp.int32)


def draw_span_start(key, part):
    key = jax.random.fold_in(key, 14)
    offsets = jax.random.randint(key, (SPANS,), 0, TOK_DEV // 4)
    return (jnp.arange(SPANS) * TOK_DEV + offsets).astype(jnp.int32)


def draw_span_end(key, part):
    key = jax.random.fold_in(key, 15)
    offsets = jax.random.randint(key, (SPANS,), 3 * TOK_DEV // 4 + 1, TOK_DEV + 1)
    return (jnp.arange(SPANS) * TOK_DEV + offsets).astype(jnp.int32)


def draw_image_owner(key, part):
    key = jax.random.fold_in(key, 16)
    steps_back = jax.random.randint(key, (SPANS,), 0, 2)
    return jnp.maximum(jnp.arange(SPANS) - steps_back, 0).astype(jnp.int32)


def steps_of(own_key, extent, shards, smallest, high):
    def one(axis_at, shards_of):
        draws = jax.random.uniform(jax.random.fold_in(jax.random.fold_in(own_key, 6), axis_at), (shards_of,), jnp.float32, smallest / len(shards), high / len(shards))
        return jnp.repeat(jnp.exp(draws), extent[axis_at] // shards_of).reshape((-1,) + (1,) * (len(extent) - axis_at - 1))

    level = one(*shards[0])
    for cut in shards[1:]:
        level = level * one(*cut)
    return level


def centred(stream_key, shape, width, most, cuts=(), held_as=jnp.bfloat16):
    level = steps_of(stream_key, shape, cuts, -0.22, 0.18) if cuts else 1.0
    values = jax.random.normal(stream_key, shape, jnp.float32) * width * level
    return jnp.minimum(jnp.maximum(values, -most), most).astype(held_as)


def setup_inputs(seed: int = 0) -> dict:
    key_of = jax.random.split(jax.random.key(seed), 8)
    return {
        "queries": draw_queries(jax.random.fold_in(key_of[7], 71), 0),
        "out_grad": centred(key_of[1], (TOKENS, HEADS * HEAD), 1.0, 6.0, ((0, 64), (1, 4))),
        "image_kv": draw_image_kv(jax.random.fold_in(key_of[7], 71), 0),
        "tiles": draw_tiles(jax.random.fold_in(key_of[7], 71), 0),
        "span_start": draw_span_start(jax.random.fold_in(key_of[7], 71), 0),
        "span_end": draw_span_end(jax.random.fold_in(key_of[7], 71), 0),
        "image_owner": draw_image_owner(jax.random.fold_in(key_of[7], 71), 0),
    }


def reference(queries, out_grad, image_kv, tiles, span_start, span_end, image_owner):
    group = HEADS // KV_HEADS
    scale = HEAD ** -0.5
    key_ids = jnp.arange(ROWS_IMG, dtype=jnp.int32)

    def reader(index):
        start = (index * TOK_DEV).astype(jnp.int32)
        query_block = lax.dynamic_slice_in_dim(queries, start, TOK_DEV, 0).astype(jnp.float32).reshape(TOK_DEV, KV_HEADS, group, HEAD)
        grad_block = lax.dynamic_slice_in_dim(out_grad, start, TOK_DEV, 0).astype(jnp.float32).reshape(TOK_DEV, KV_HEADS, group, HEAD)
        source = image_owner[index].astype(jnp.int32)
        pair = lax.dynamic_index_in_dim(image_kv, source, 0, keepdims=False).astype(jnp.float32)
        key_rows = pair[0].reshape(ROWS_IMG, KV_HEADS, HEAD)
        value_rows = pair[1].reshape(ROWS_IMG, KV_HEADS, HEAD)
        token_ids = start + jnp.arange(TOK_DEV, dtype=jnp.int32)
        row_valid = (token_ids >= span_start[index]) & (token_ids < span_end[index])
        key_valid = key_ids < tiles[source] * TILE_ROWS
        valid = row_valid[:, None] & key_valid[None, :]
        scores = jnp.einsum('tkgd,rkd->kgtr', query_block, key_rows) * scale
        masked = jnp.where(valid, scores, -jnp.inf)
        has_key = jnp.any(valid, axis=1)[:, None]
        top = jnp.where(has_key, jnp.max(masked, axis=-1, keepdims=True), 0.0)
        expo = jnp.where(valid, jnp.exp(scores - top), 0.0)
        total = jnp.sum(expo, axis=-1, keepdims=True)
        probs = expo / jnp.where(has_key, total, 1.0)
        probs_low = lax.optimization_barrier(probs.astype(jnp.bfloat16)).astype(jnp.float32)
        grad_probs = jnp.einsum('tkgd,rkd->kgtr', grad_block, value_rows)
        weighted = jnp.sum(probs * grad_probs, axis=-1, keepdims=True)
        grad_scores = lax.optimization_barrier((probs * (grad_probs - weighted)).astype(jnp.bfloat16)).astype(jnp.float32)
        grad_query = (jnp.einsum('kgtr,rkd->tkgd', grad_scores, key_rows) * scale).reshape(TOK_DEV, HEADS * HEAD).astype(jnp.bfloat16)
        grad_key = jnp.einsum('kgtr,tkgd->rkd', grad_scores, query_block) * scale
        grad_value = jnp.einsum('kgtr,tkgd->rkd', probs_low, grad_block)
        part = jnp.stack([grad_key.reshape(ROWS_IMG, KV_HEADS * HEAD), grad_value.reshape(ROWS_IMG, KV_HEADS * HEAD)])
        return grad_query, part

    def step(previous, index):
        grad_query, part = reader(index)
        source = image_owner[index]
        finished = previous + jnp.where(source == index - 1, part, jnp.zeros_like(part))
        keep = jnp.where(source == index, part, jnp.zeros_like(part))
        return keep, (grad_query, finished.astype(jnp.bfloat16))

    start_carry = jnp.zeros((2, ROWS_IMG, KV_HEADS * HEAD), jnp.float32)
    last, (query_grads, finished_all) = lax.scan(step, start_carry, jnp.arange(SPANS, dtype=jnp.int32))
    grad_image_kv = jnp.concatenate([finished_all[1:], last.astype(jnp.bfloat16)[None]], axis=0)
    return query_grads.reshape(TOKENS, HEADS * HEAD), grad_image_kv
```

```python
import jax
import jax.numpy as jnp
from jax import lax
from jax.experimental import pallas as pl
from jax.experimental.pallas import tpu as pltpu
from jax.sharding import PartitionSpec as P

HEAD = 128
GROUP = 8
TILE_ROWS = 1601
TILE_PAD = 1616
MAX_TILES = 4
TOK = 128
BLOCK_TOK = 32
COLS = BLOCK_TOK * GROUP
SCALE = HEAD**-0.5
LOG2 = SCALE * 1.4426950408889634
SAFE = 2.0**60
F32 = jnp.float32
BF16 = jnp.bfloat16


def dot_last(a, b):
    return lax.dot_general(a, b, (((1,), (1,)), ((), ())), preferred_element_type=F32)


def dot(a, b):
    return jnp.dot(a, b, preferred_element_type=F32)


def by8(x):
    return x.reshape(x.shape[0] // 8, 8, x.shape[1])


def backward_kernel(
    place, tiles, starts, ends, owner, qo, go, qi, gi, kv,
    dqo, dqi, out,
    e_s, p_s, ak, av, inter, dq_s, m_s, st_s, qb, gb, qf, gf, kt,
):
    here = place[0]
    last = starts.shape[0] - 1
    after = jnp.minimum(here + 1, last)
    own = owner[here] == here
    incoming = (here < last) & (owner[after] == here)
    live_tiles = tiles[here]

    def clear(t, _):
        ak[t] = jnp.zeros((TILE_PAD, HEAD), F32)
        av[t] = jnp.zeros((TILE_PAD, HEAD), F32)
        kt[t] = kv[0, t].T
        return 0

    lax.fori_loop(0, live_tiles, clear, 0)

    def block(i, q_ref, g_ref, dq_ref, span):
        first = pl.multiple_of(i * BLOCK_TOK, BLOCK_TOK)
        token = span * TOK + first + lax.broadcasted_iota(jnp.int32, (BLOCK_TOK, HEAD), 0)
        alive = (token >= starts[span]) & (token < ends[span])
        for h in range(GROUP):
            rows = slice(h * BLOCK_TOK, (h + 1) * BLOCK_TOK)
            cols = slice(h * HEAD, (h + 1) * HEAD)
            qh = q_ref[pl.ds(first, BLOCK_TOK), cols].astype(F32)
            gh = g_ref[pl.ds(first, BLOCK_TOK), cols].astype(F32)
            qb[rows, :] = jnp.where(alive, qh, 0.0).astype(BF16)
            gb[rows, :] = jnp.where(alive, gh, 0.0).astype(BF16)

        keep = lax.broadcasted_iota(jnp.int32, (16, COLS), 0) < 1

        def first_pass(t, sums):
            total, dotted = sums
            top = m_s[...] * LOG2
            s = dot_last(kv[0, t], qb[...])
            p = dot_last(kv[1, t], gb[...])
            e = jnp.exp2(by8(s) * LOG2 - top).reshape(TILE_PAD, COLS)
            full = TILE_PAD - 16
            e = jnp.concatenate([e[:full], jnp.where(keep, e[full:], 0.0)], axis=0)
            total += jnp.sum(by8(e), 0)
            dotted += jnp.sum(by8(e * p), 0)
            e_s[t] = e
            p_s[t] = p
            return total, dotted

        def sweep():
            zero = jnp.zeros((8, COLS), F32)
            total, dotted = lax.fori_loop(0, live_tiles, first_pass, (zero, zero))
            total = jnp.sum(total, 0, keepdims=True)
            dotted = jnp.sum(dotted, 0, keepdims=True)
            st_s[0:8] = jnp.broadcast_to(total, (8, COLS))
            st_s[8:16] = jnp.broadcast_to(dotted, (8, COLS))
            inside = (total > 1.0 / SAFE) & (total < SAFE)
            return jnp.min(jnp.where(inside, 1.0, 0.0)) > 0.5

        m_s[...] = jnp.zeros((8, COLS), F32)
        fine = sweep()

        @pl.when(jnp.logical_not(fine))
        def _():
            def peak(t, top):
                s = dot_last(kv[0, t], qb[...])
                full = TILE_PAD - 16
                ending = jnp.where(keep, s[full:], -jnp.inf)
                most = jnp.maximum(jnp.max(by8(s[:full]), 0), jnp.max(by8(ending), 0))
                return jnp.maximum(top, most)

            top = lax.fori_loop(0, live_tiles, peak, jnp.full((8, COLS), -jnp.inf, F32))
            m_s[...] = jnp.broadcast_to(jnp.max(top, 0, keepdims=True), (8, COLS))
            sweep()

        inverse = 1.0 / st_s[0:1]
        mean = st_s[8:16] * (1.0 / st_s[0:8])
        column = jnp.broadcast_to(inverse, (HEAD, COLS)).T
        qf[...] = (qb[...].astype(F32) * column).astype(BF16)
        gf[...] = (gb[...].astype(F32) * column).astype(BF16)
        dq_s[...] = jnp.zeros_like(dq_s)

        def second_pass(t, _):
            e = e_s[t]
            low = e.astype(BF16)
            ds = (by8(e) * (by8(p_s[t]) - mean)).reshape(TILE_PAD, COLS).astype(BF16)
            av[t] += dot(low, gf[...])
            ak[t] += dot(ds, qf[...])
            dq_s[...] += dot(kt[t], ds)
            return 0

        lax.fori_loop(0, live_tiles, second_pass, 0)
        dq = (dq_s[...].T * (column * SCALE)).astype(BF16)
        for h in range(GROUP):
            rows = slice(h * BLOCK_TOK, (h + 1) * BLOCK_TOK)
            cols = slice(h * HEAD, (h + 1) * HEAD)
            dq_ref[pl.ds(first, BLOCK_TOK), cols] = dq[rows]

    blocks = TOK // BLOCK_TOK

    def both(i, _):
        pl.when(i < blocks)(lambda: block(i, qo, go, dqo, here))
        pl.when(i >= blocks)(lambda: block(i - blocks, qi, gi, dqi, after))
        return 0

    @pl.when(jnp.logical_not(own))
    def _():
        dqo[...] = jnp.zeros_like(dqo)

    @pl.when(jnp.logical_not(incoming))
    def _():
        dqi[...] = jnp.zeros_like(dqi)

    lax.fori_loop(jnp.where(own, 0, blocks), jnp.where(incoming, 2 * blocks, blocks), both, 0)

    for t in range(MAX_TILES):
        base = 2 * TILE_ROWS * t
        alive = (t < live_tiles) & (own | incoming)

        @pl.when(alive)
        def _():
            inter[pl.ds(base, TILE_ROWS, stride=2), :] = ak[t, :TILE_ROWS, :] * SCALE
            inter[pl.ds(base + 1, TILE_ROWS, stride=2), :] = av[t, :TILE_ROWS, :]

        @pl.when(jnp.logical_not(alive))
        def _():
            inter[base : base + 2 * TILE_ROWS, :] = jnp.zeros((2 * TILE_ROWS, HEAD), F32)

    out[...] = inter[...].astype(BF16)


def backward(place, tiles, starts, ends, owner, qo, go, qi, gi, kv):
    vmem = pl.BlockSpec(memory_space=pltpu.VMEM)
    smem = pl.BlockSpec(memory_space=pltpu.SMEM)
    big = (MAX_TILES, TILE_PAD, COLS)
    acc = (MAX_TILES, TILE_PAD, HEAD)
    return pl.pallas_call(
        backward_kernel,
        out_shape=[
            jax.ShapeDtypeStruct(qo.shape, BF16),
            jax.ShapeDtypeStruct(qo.shape, BF16),
            jax.ShapeDtypeStruct((2 * TILE_ROWS * MAX_TILES, HEAD), BF16),
        ],
        in_specs=[smem] * 5 + [vmem] * 5,
        out_specs=[vmem] * 3,
        scratch_shapes=[
            pltpu.VMEM(big, F32),
            pltpu.VMEM(big, F32),
            pltpu.VMEM(acc, F32),
            pltpu.VMEM(acc, F32),
            pltpu.VMEM((2 * TILE_ROWS * MAX_TILES, HEAD), F32),
            pltpu.VMEM((HEAD, COLS), F32),
            pltpu.VMEM((8, COLS), F32),
            pltpu.VMEM((16, COLS), F32),
        ]
        + [pltpu.VMEM((COLS, HEAD), BF16)] * 4
        + [pltpu.VMEM((MAX_TILES, HEAD, TILE_PAD), BF16)],
        compiler_params=pltpu.CompilerParams(vmem_limit_bytes=60 * 2**20),
    )(place, tiles, starts, ends, owner, qo, go, qi, gi, kv)


def shards(queries, out_grad, image_kv, tiles, span_start, span_end, image_owner):
    spans = lax.axis_size("ctx")
    place = lax.axis_index("ctx").astype(jnp.int32).reshape(1)
    earlier = [(i, i - 1) for i in range(1, spans)]
    later = [(i, i + 1) for i in range(spans - 1)]
    queries_in = lax.ppermute(queries, "ctx", earlier)
    grads_in = lax.ppermute(out_grad, "ctx", earlier)
    kv = image_kv.reshape(2, MAX_TILES, TILE_ROWS, HEAD)
    kv = jnp.pad(kv, ((0, 0), (0, 0), (0, TILE_PAD - TILE_ROWS), (0, 0)))
    own, other, image = backward(
        place, tiles, span_start, span_end, image_owner, queries, out_grad, queries_in, grads_in, kv
    )
    returned = lax.ppermute(other, "ctx", later)
    grad_queries = own + returned
    grad_kv = image.reshape(1, MAX_TILES * TILE_ROWS, 2, HEAD).transpose(0, 2, 1, 3)
    return grad_queries, grad_kv


def solution(mesh):
    return jax.shard_map(
        shards,
        mesh=mesh,
        in_specs=(P("ctx", "tp"), P("ctx", "tp"), P("ctx", None, None, "tp"), P(), P(), P(), P()),
        out_specs=(P("ctx", "tp"), P("ctx", None, None, "tp")),
        check_vma=False,
    )
```

```python
import jax
import jax.numpy as jnp
from jax import lax
from jax.experimental import pallas as pl
from jax.experimental.pallas import tpu as pltpu
from jax.sharding import PartitionSpec as P

HEAD = 128
GROUP = 8
TILE_ROWS = 1601
TILE_PAD = 1616
MAX_TILES = 4
TOK = 128
BLOCK_TOK = 32
COLS = BLOCK_TOK * GROUP
SCALE = HEAD**-0.5
LOG2 = SCALE * 1.4426950408889634
SAFE = 2.0**60
F32 = jnp.float32
BF16 = jnp.bfloat16


def dot_last(a, b):
    return lax.dot_general(a, b, (((1,), (1,)), ((), ())), preferred_element_type=F32)


def dot(a, b):
    return jnp.dot(a, b, preferred_element_type=F32)


def by8(x):
    return x.reshape(x.shape[0] // 8, 8, x.shape[1])


def backward_kernel(
    place, tiles, starts, ends, owner, qo, go, qi, gi, kv,
    dqo, dqi, out,
    e0, e1, p0, p1, ak, av, inter, dq_s, sums0, sums1, qs, qb, gb, qf0, qf1, gf0, gf1, qc, gc, dqc, kt,
):
    e_s, p_s, sums, qf, gf = (e0, e1), (p0, p1), (sums0, sums1), (qf0, qf1), (gf0, gf1)
    here = place[0]
    last = starts.shape[0] - 1
    after = jnp.minimum(here + 1, last)
    own = owner[here] == here
    incoming = (here < last) & (owner[after] == here)
    live_tiles = tiles[here]
    full = TILE_PAD - 16
    own_first = starts[here] - here * TOK
    in_first = starts[after] - after * TOK
    own_many = jnp.where(own, ends[here] - starts[here], 0)
    in_many = jnp.where(incoming, ends[after] - starts[after], 0)
    count = (own_many + in_many + BLOCK_TOK - 1) // BLOCK_TOK

    def clear(t, _):
        ak[t] = jnp.zeros((TILE_PAD, HEAD), F32)
        av[t] = jnp.zeros((TILE_PAD, HEAD), F32)
        kt[t] = kv[0, t].T
        return 0

    lax.fori_loop(0, live_tiles, clear, 0)

    def places(shape, packed_dim):
        packed = lax.broadcasted_iota(jnp.int32, shape, packed_dim)
        token = lax.broadcasted_iota(jnp.int32, shape, 1 - packed_dim)
        from_own = (packed < own_many) & (token == packed + own_first)
        moved = packed - own_many
        from_in = (moved >= 0) & (moved < in_many) & (token == moved + in_first)
        return jnp.where(from_own, 1.0, 0.0).astype(BF16), jnp.where(from_in, 1.0, 0.0).astype(BF16)

    @pl.when(count > 0)
    def _():
        take_own, take_in = places((2 * TOK, TOK), 0)
        take = jnp.concatenate([take_own, take_in], axis=1)
        qc[...] = dot(take, jnp.concatenate([qo[...], qi[...]], axis=0))
        gc[...] = dot(take, jnp.concatenate([go[...], gi[...]], axis=0))
        dqc[...] = jnp.zeros_like(dqc)

    def prepare(i, _):
        packed = pl.ds(pl.multiple_of(i * BLOCK_TOK, BLOCK_TOK), BLOCK_TOK)
        for h in range(GROUP):
            rows = slice(h * BLOCK_TOK, (h + 1) * BLOCK_TOK)
            cols = slice(h * HEAD, (h + 1) * HEAD)
            q = qc[packed, cols]
            scaled = q * LOG2
            high = scaled.astype(BF16)
            qs[i, rows, :HEAD] = high
            qs[i, rows, HEAD:] = (scaled - high.astype(F32)).astype(BF16)
            qb[i, rows, :] = q.astype(BF16)
            gb[i, rows, :] = gc[packed, cols].astype(BF16)
        return 0

    lax.fori_loop(0, count, prepare, 0)

    keep = lax.broadcasted_iota(jnp.int32, (16, COLS), 0) < 1
    zero = jnp.zeros((8, COLS), F32)

    def first(n, t, at, top, total, dotted):
        k = kv[0, t]
        s = dot_last(jnp.concatenate([k, k], axis=1), qs[n])
        if top is not None:
            s = (by8(s) - top).reshape(TILE_PAD, COLS)
        p = dot_last(kv[1, t], gb[n])
        e = jnp.exp2(s)
        e = jnp.concatenate([e[:full], jnp.where(keep, e[full:], 0.0)], axis=0)
        total += jnp.sum(by8(e), 0)
        dotted += jnp.sum(by8(e * p), 0)
        e_s[at][t] = e
        p_s[at][t] = p
        return total, dotted

    def second(t, at):
        mean = sums[at][8:16]
        e = e_s[at][t]
        low = e.astype(BF16)
        ds = (by8(e) * (by8(p_s[at][t]) - mean)).reshape(TILE_PAD, COLS).astype(BF16)
        av[t] += dot(low, gf[at][...])
        ak[t] += dot(ds, qf[at][...])
        dq_s[...] += dot(kt[t], ds)

    def settle(n, at, total, dotted):
        total = jnp.sum(total, 0, keepdims=True)
        dotted = jnp.sum(dotted, 0, keepdims=True)
        sums[at][0:8] = jnp.broadcast_to(total, (8, COLS))
        sums[at][8:16] = jnp.broadcast_to(dotted, (8, COLS))
        inside = (total > 1.0 / SAFE) & (total < SAFE)

        @pl.when(jnp.min(jnp.where(inside, 1.0, 0.0)) < 0.5)
        def _():
            def peak(t, top):
                k = kv[0, t]
                s = dot_last(jnp.concatenate([k, k], axis=1), qs[n])
                ending = jnp.where(keep, s[full:], -jnp.inf)
                return jnp.maximum(top, jnp.maximum(jnp.max(by8(s[:full]), 0), jnp.max(by8(ending), 0)))

            top = lax.fori_loop(0, live_tiles, peak, jnp.full((8, COLS), -jnp.inf, F32))
            top = jnp.broadcast_to(jnp.max(top, 0, keepdims=True), (8, COLS))
            total, dotted = lax.fori_loop(0, live_tiles, lambda t, c: first(n, t, at, top, *c), (zero, zero))
            sums[at][0:8] = jnp.broadcast_to(jnp.sum(total, 0, keepdims=True), (8, COLS))
            sums[at][8:16] = jnp.broadcast_to(jnp.sum(dotted, 0, keepdims=True), (8, COLS))

        inverse = 1.0 / sums[at][0:8]
        sums[at][8:16] = sums[at][8:16] * inverse
        column = jnp.broadcast_to(inverse[0:1], (HEAD, COLS)).T
        qf[at][...] = (qb[n].astype(F32) * column).astype(BF16)
        gf[at][...] = (gb[n].astype(F32) * column).astype(BF16)

    def finish(n, at):
        inverse = 1.0 / sums[at][0:1]
        column = jnp.broadcast_to(inverse * SCALE, (HEAD, COLS))
        dq = (dq_s[...] * column).T.astype(BF16)
        packed = pl.ds(pl.multiple_of(n * BLOCK_TOK, BLOCK_TOK), BLOCK_TOK)
        for h in range(GROUP):
            dqc[packed, h * HEAD : (h + 1) * HEAD] = dq[h * BLOCK_TOK : (h + 1) * BLOCK_TOK]
        dq_s[...] = jnp.zeros_like(dq_s)

    def over_tiles(steps, c):
        def narrow(c):
            return lax.fori_loop(0, live_tiles, lambda t, c: steps(t, c, 1), c)

        def wide(c):
            return steps(0, c, MAX_TILES)

        return lax.cond(live_tiles == MAX_TILES, wide, narrow, c)

    def lead(n, at):
        def steps(t, c, width):
            for u in range(width):
                c = first(n, t + u, at, None, *c)
            return c

        total, dotted = over_tiles(steps, (zero, zero))
        settle(n, at, total, dotted)

    def both(n, at):
        def steps(t, c, width):
            for u in range(width):
                c = first(n, t + u, at, None, *c)
            for u in range(width):
                second(t + u, 1 - at)
            return c

        total, dotted = over_tiles(steps, (zero, zero))
        finish(n - 1, 1 - at)
        settle(n, at, total, dotted)

    def trail(n, at):
        def steps(t, c, width):
            for u in range(width):
                second(t + u, at)
            return c

        over_tiles(steps, 0)
        finish(n, at)

    @pl.when(count > 0)
    def _():
        dq_s[...] = jnp.zeros_like(dq_s)
        lead(0, 0)

        def pair(j, _):
            both(2 * j + 1, 1)
            pl.when(2 * j + 2 < count)(lambda: both(2 * j + 2, 0))
            return 0

        lax.fori_loop(0, count // 2, pair, 0)
        pl.when(lax.rem(count, 2) == 0)(lambda: trail(count - 1, 1))
        pl.when(lax.rem(count, 2) == 1)(lambda: trail(count - 1, 0))
        give_own, give_in = places((TOK, 2 * TOK), 1)
        dqo[...] = dot(give_own, dqc[...]).astype(BF16)
        dqi[...] = dot(give_in, dqc[...]).astype(BF16)

    @pl.when(count == 0)
    def _():
        dqo[...] = jnp.zeros_like(dqo)
        dqi[...] = jnp.zeros_like(dqi)

    for t in range(MAX_TILES):
        base = 2 * TILE_ROWS * t
        alive = (t < live_tiles) & (count > 0)

        @pl.when(alive)
        def _():
            inter[pl.ds(base, TILE_ROWS, stride=2), :] = ak[t, :TILE_ROWS, :] * SCALE
            inter[pl.ds(base + 1, TILE_ROWS, stride=2), :] = av[t, :TILE_ROWS, :]

        @pl.when(jnp.logical_not(alive))
        def _():
            inter[base : base + 2 * TILE_ROWS, :] = jnp.zeros((2 * TILE_ROWS, HEAD), F32)

    out[...] = inter[...].astype(BF16)


def backward(place, tiles, starts, ends, owner, qo, go, qi, gi, kv):
    vmem = pl.BlockSpec(memory_space=pltpu.VMEM)
    smem = pl.BlockSpec(memory_space=pltpu.SMEM)
    big = (MAX_TILES, TILE_PAD, COLS)
    acc = (MAX_TILES, TILE_PAD, HEAD)
    blocks = 2 * TOK // BLOCK_TOK
    return pl.pallas_call(
        backward_kernel,
        out_shape=[
            jax.ShapeDtypeStruct(qo.shape, BF16),
            jax.ShapeDtypeStruct(qo.shape, BF16),
            jax.ShapeDtypeStruct((2 * TILE_ROWS * MAX_TILES, HEAD), BF16),
        ],
        in_specs=[smem] * 5 + [vmem] * 5,
        out_specs=[vmem] * 3,
        scratch_shapes=[pltpu.VMEM(big, F32)] * 4
        + [pltpu.VMEM(acc, F32)] * 2
        + [
            pltpu.VMEM((2 * TILE_ROWS * MAX_TILES, HEAD), F32),
            pltpu.VMEM((HEAD, COLS), F32),
            pltpu.VMEM((16, COLS), F32),
            pltpu.VMEM((16, COLS), F32),
            pltpu.VMEM((blocks, COLS, 2 * HEAD), BF16),
            pltpu.VMEM((blocks, COLS, HEAD), BF16),
            pltpu.VMEM((blocks, COLS, HEAD), BF16),
        ]
        + [pltpu.VMEM((COLS, HEAD), BF16)] * 4
        + [pltpu.VMEM((2 * TOK, GROUP * HEAD), F32)] * 2
        + [pltpu.VMEM((2 * TOK, GROUP * HEAD), BF16), pltpu.VMEM((MAX_TILES, HEAD, TILE_PAD), BF16)],
        compiler_params=pltpu.CompilerParams(vmem_limit_bytes=60 * 2**20),
    )(place, tiles, starts, ends, owner, qo, go, qi, gi, kv)


def shards(queries, out_grad, image_kv, tiles, span_start, span_end, image_owner):
    spans = lax.axis_size("ctx")
    place = lax.axis_index("ctx").astype(jnp.int32).reshape(1)
    earlier = [(i, i - 1) for i in range(1, spans)]
    later = [(i, i + 1) for i in range(spans - 1)]
    queries_in = lax.ppermute(queries, "ctx", earlier)
    grads_in = lax.ppermute(out_grad, "ctx", earlier)
    kv = image_kv.reshape(2, MAX_TILES, TILE_ROWS, HEAD)
    kv = jnp.pad(kv, ((0, 0), (0, 0), (0, TILE_PAD - TILE_ROWS), (0, 0)))
    own, other, image = backward(
        place, tiles, span_start, span_end, image_owner, queries, out_grad, queries_in, grads_in, kv
    )
    returned = lax.ppermute(other, "ctx", later)
    grad_queries = own + returned
    grad_kv = image.reshape(1, MAX_TILES * TILE_ROWS, 2, HEAD).transpose(0, 2, 1, 3)
    return grad_queries, grad_kv


def solution(mesh):
    return jax.shard_map(
        shards,
        mesh=mesh,
        in_specs=(P("ctx", "tp"), P("ctx", "tp"), P("ctx", None, None, "tp"), P(), P(), P(), P()),
        out_specs=(P("ctx", "tp"), P("ctx", None, None, "tp")),
        check_vma=False,
    )
```

```python
import jax
import jax.numpy as jnp
from jax import lax
from jax.experimental import pallas as pl
from jax.experimental.pallas import tpu as pltpu
from jax.sharding import PartitionSpec as P

HEAD = 128
GROUP = 8
TILE_ROWS = 1601
TILE_PAD = 1616
MAX_TILES = 4
TOK = 128
BLOCK_TOK = 32
COLS = BLOCK_TOK * GROUP
SCALE = HEAD**-0.5
LOG2 = SCALE * 1.4426950408889634
SAFE = 2.0**60
F32 = jnp.float32
BF16 = jnp.bfloat16


def dot_last(a, b):
    return lax.dot_general(a, b, (((1,), (1,)), ((), ())), preferred_element_type=F32)


def dot(a, b):
    return jnp.dot(a, b, preferred_element_type=F32)


def by8(x):
    return x.reshape(x.shape[0] // 8, 8, x.shape[1])


def backward_kernel(
    place, tiles, starts, ends, owner, qo, go, moved_in, kv_far,
    dqo, dqi, out_far,
    e0, e1, p0, p1, ak, av, dq_s, sums0, sums1, safe_s, qs, qb, gb, qf0, qf1, gf0, gf1, qc, gc, dqc, kt,
    kv, out, in_sem, out_sem,
):
    e_s, p_s, sums, qf, gf = (e0, e1), (p0, p1), (sums0, sums1), (qf0, qf1), (gf0, gf1)
    here = place[0]
    last = starts.shape[0] - 1
    after = jnp.minimum(here + 1, last)
    own = owner[here] == here
    incoming = (here < last) & (owner[after] == here)
    live_tiles = tiles[here]
    full = TILE_PAD - 16
    own_first = starts[here] - here * TOK
    in_first = starts[after] - after * TOK
    own_many = jnp.where(own, ends[here] - starts[here], 0)
    in_many = jnp.where(incoming, ends[after] - starts[after], 0)
    count = (own_many + in_many + BLOCK_TOK - 1) // BLOCK_TOK

    arriving = [
        [pltpu.make_async_copy(kv_far.at[i, t], kv.at[i, t], in_sem.at[i, t]) for t in range(MAX_TILES)]
        for i in range(2)
    ]
    for i in range(2):
        for t in range(MAX_TILES):
            arriving[i][t].start()

    def places(shape, packed_dim):
        packed = lax.broadcasted_iota(jnp.int32, shape, packed_dim)
        token = lax.broadcasted_iota(jnp.int32, shape, 1 - packed_dim)
        from_own = (packed < own_many) & (token == packed + own_first)
        moved = packed - own_many
        from_in = (moved >= 0) & (moved < in_many) & (token == moved + in_first)
        return jnp.where(from_own, 1.0, 0.0).astype(BF16), jnp.where(from_in, 1.0, 0.0).astype(BF16)

    @pl.when(count > 0)
    def _():
        take_own, take_in = places((2 * TOK, TOK), 0)
        take = jnp.concatenate([take_own, take_in], axis=1)
        qc[...] = dot(take, jnp.concatenate([qo[...], moved_in[0]], axis=0))
        gc[...] = dot(take, jnp.concatenate([go[...], moved_in[1]], axis=0))
        dqc[...] = jnp.zeros_like(dqc)
        safe_s[...] = jnp.ones_like(safe_s)

    def prepare(i, _):
        packed = pl.ds(pl.multiple_of(i * BLOCK_TOK, BLOCK_TOK), BLOCK_TOK)
        for h in range(GROUP):
            rows = slice(h * BLOCK_TOK, (h + 1) * BLOCK_TOK)
            cols = slice(h * HEAD, (h + 1) * HEAD)
            q = qc[packed, cols]
            scaled = q * LOG2
            high = scaled.astype(BF16)
            qs[i, rows, :HEAD] = high
            qs[i, rows, HEAD:] = (scaled - high.astype(F32)).astype(BF16)
            qb[i, rows, :] = q.astype(BF16)
            gb[i, rows, :] = gc[packed, cols].astype(BF16)
        return 0

    lax.fori_loop(0, count, prepare, 0)
    for i in range(2):
        for t in range(MAX_TILES):
            arriving[i][t].wait()

    def clear(t, _):
        ak[t] = jnp.zeros((TILE_PAD, HEAD), F32)
        av[t] = jnp.zeros((TILE_PAD, HEAD), F32)
        kt[t] = kv[0, t].T
        return 0

    lax.fori_loop(0, live_tiles, clear, 0)

    keep = lax.broadcasted_iota(jnp.int32, (16, COLS), 0) < 1
    zero = jnp.zeros((8, COLS), F32)

    def first(n, t, at, top, total, dotted):
        k = kv[0, t]
        s = dot_last(jnp.concatenate([k, k], axis=1), qs[n])
        if top is not None:
            s = (by8(s) - top).reshape(TILE_PAD, COLS)
        p = dot_last(kv[1, t], gb[n])
        e = jnp.exp2(s)
        e = jnp.concatenate([e[:full], jnp.where(keep, e[full:], 0.0)], axis=0)
        total += jnp.sum(by8(e), 0)
        dotted += jnp.sum(by8(e * p), 0)
        e_s[at][t] = e
        p_s[at][t] = p
        return total, dotted

    def second(t, at):
        mean = sums[at][8:16]
        e = e_s[at][t]
        low = e.astype(BF16)
        ds = (by8(e) * (by8(p_s[at][t]) - mean)).reshape(TILE_PAD, COLS).astype(BF16)
        av[t] += dot(low, gf[at][...])
        ak[t] += dot(ds, qf[at][...])
        dq_s[...] += dot(kt[t], ds)

    def settle(n, at, total, dotted):
        total = jnp.sum(total, 0, keepdims=True)
        dotted = jnp.sum(dotted, 0, keepdims=True)
        inside = (total > 1.0 / SAFE) & (total < SAFE)
        safe_s[...] = jnp.minimum(safe_s[...], jnp.where(inside, 1.0, 0.0))
        inverse = 1.0 / total
        sums[at][0:8] = jnp.broadcast_to(inverse, (8, COLS))
        sums[at][8:16] = jnp.broadcast_to(dotted * inverse, (8, COLS))
        column = jnp.broadcast_to(inverse, (HEAD, COLS)).T
        qf[at][...] = (qb[n].astype(F32) * column).astype(BF16)
        gf[at][...] = (gb[n].astype(F32) * column).astype(BF16)

    def finish(n, at):
        column = jnp.broadcast_to(sums[at][0:1] * SCALE, (HEAD, COLS))
        dq = (dq_s[...] * column).T.astype(BF16)
        packed = pl.ds(pl.multiple_of(n * BLOCK_TOK, BLOCK_TOK), BLOCK_TOK)
        for h in range(GROUP):
            dqc[packed, h * HEAD : (h + 1) * HEAD] = dq[h * BLOCK_TOK : (h + 1) * BLOCK_TOK]
        dq_s[...] = jnp.zeros_like(dq_s)

    def over_tiles(wide, steps, c):
        if wide:
            return steps(0, c, MAX_TILES)
        return lax.fori_loop(0, live_tiles, lambda t, c: steps(t, c, 1), c)

    def lead(wide, n, at, top=None):
        def steps(t, c, width):
            for u in range(width):
                c = first(n, t + u, at, top, *c)
            return c

        total, dotted = over_tiles(wide, steps, (zero, zero))
        settle(n, at, total, dotted)

    def both(wide, n, at):
        def steps(t, c, width):
            for u in range(width):
                c = first(n, t + u, at, None, *c)
            for u in range(width):
                second(t + u, 1 - at)
            return c

        total, dotted = over_tiles(wide, steps, (zero, zero))
        finish(n - 1, 1 - at)
        settle(n, at, total, dotted)

    def trail(wide, n, at):
        def steps(t, c, width):
            for u in range(width):
                second(t + u, at)
            return c

        over_tiles(wide, steps, 0)
        finish(n, at)

    def pipeline(wide):
        lead(wide, 0, 0)

        def pair(j, _):
            both(wide, 2 * j + 1, 1)
            pl.when(2 * j + 2 < count)(lambda: both(wide, 2 * j + 2, 0))
            return 0

        lax.fori_loop(0, count // 2, pair, 0)
        pl.when(lax.rem(count, 2) == 0)(lambda: trail(wide, count - 1, 1))
        pl.when(lax.rem(count, 2) == 1)(lambda: trail(wide, count - 1, 0))

    def careful(n, _):
        def peak(t, top):
            k = kv[0, t]
            s = dot_last(jnp.concatenate([k, k], axis=1), qs[n])
            ending = jnp.where(keep, s[full:], -jnp.inf)
            return jnp.maximum(top, jnp.maximum(jnp.max(by8(s[:full]), 0), jnp.max(by8(ending), 0)))

        top = lax.fori_loop(0, live_tiles, peak, jnp.full((8, COLS), -jnp.inf, F32))
        top = jnp.broadcast_to(jnp.max(top, 0, keepdims=True), (8, COLS))
        lead(False, n, 0, top)
        trail(False, n, 0)
        return 0

    @pl.when(count > 0)
    def _():
        dq_s[...] = jnp.zeros_like(dq_s)
        pl.when(live_tiles == MAX_TILES)(lambda: pipeline(True))
        pl.when(live_tiles != MAX_TILES)(lambda: pipeline(False))

        @pl.when(jnp.min(safe_s[...]) < 0.5)
        def _():
            lax.fori_loop(0, live_tiles, clear, 0)
            dq_s[...] = jnp.zeros_like(dq_s)
            lax.fori_loop(0, count, careful, 0)

    leaving = [
        [pltpu.make_async_copy(out.at[i, t], out_far.at[i, t], out_sem.at[i, t]) for t in range(MAX_TILES)]
        for i in range(2)
    ]
    for t in range(MAX_TILES):
        alive = (t < live_tiles) & (count > 0)

        @pl.when(alive)
        def _():
            out[0, t] = (ak[t] * SCALE).astype(BF16)
            out[1, t] = av[t].astype(BF16)

        @pl.when(jnp.logical_not(alive))
        def _():
            out[0, t] = jnp.zeros((TILE_PAD, HEAD), BF16)
            out[1, t] = jnp.zeros((TILE_PAD, HEAD), BF16)

        leaving[0][t].start()
        leaving[1][t].start()

    @pl.when(count > 0)
    def _():
        give_own, give_in = places((TOK, 2 * TOK), 1)
        dqo[...] = dot(give_own, dqc[...]).astype(BF16)
        dqi[...] = dot(give_in, dqc[...]).astype(BF16)

    @pl.when(count == 0)
    def _():
        dqo[...] = jnp.zeros_like(dqo)
        dqi[...] = jnp.zeros_like(dqi)

    for t in range(MAX_TILES):
        leaving[0][t].wait()
        leaving[1][t].wait()


def interleave_kernel(parts, out, inter):
    for t in range(MAX_TILES):
        base = 2 * TILE_ROWS * t
        for i in range(2):
            inter[pl.ds(base + i, TILE_ROWS, stride=2), :] = parts[i, t].astype(F32)[:TILE_ROWS]
    out[...] = inter[...].astype(BF16)


def interleave(parts):
    rows = 2 * TILE_ROWS * MAX_TILES
    vmem = pl.BlockSpec(memory_space=pltpu.VMEM)
    return pl.pallas_call(
        interleave_kernel,
        out_shape=jax.ShapeDtypeStruct((rows, HEAD), BF16),
        in_specs=[vmem],
        out_specs=vmem,
        scratch_shapes=[pltpu.VMEM((rows, HEAD), F32)],
        compiler_params=pltpu.CompilerParams(vmem_limit_bytes=32 * 2**20),
    )(parts)


def backward(place, tiles, starts, ends, owner, qo, go, moved_in, kv):
    vmem = pl.BlockSpec(memory_space=pltpu.VMEM)
    smem = pl.BlockSpec(memory_space=pltpu.SMEM)
    far = pl.BlockSpec(memory_space=pl.ANY)
    big = (MAX_TILES, TILE_PAD, COLS)
    acc = (MAX_TILES, TILE_PAD, HEAD)
    blocks = 2 * TOK // BLOCK_TOK
    return pl.pallas_call(
        backward_kernel,
        out_shape=[
            jax.ShapeDtypeStruct(qo.shape, BF16),
            jax.ShapeDtypeStruct(qo.shape, BF16),
            jax.ShapeDtypeStruct(kv.shape, BF16),
        ],
        in_specs=[smem] * 5 + [vmem] * 3 + [far],
        out_specs=[vmem] * 2 + [far],
        scratch_shapes=[pltpu.VMEM(big, F32)] * 4
        + [pltpu.VMEM(acc, F32)] * 2
        + [
            pltpu.VMEM((HEAD, COLS), F32),
            pltpu.VMEM((16, COLS), F32),
            pltpu.VMEM((16, COLS), F32),
            pltpu.VMEM((8, COLS), F32),
            pltpu.VMEM((blocks, COLS, 2 * HEAD), BF16),
            pltpu.VMEM((blocks, COLS, HEAD), BF16),
            pltpu.VMEM((blocks, COLS, HEAD), BF16),
        ]
        + [pltpu.VMEM((COLS, HEAD), BF16)] * 4
        + [pltpu.VMEM((2 * TOK, GROUP * HEAD), F32)] * 2
        + [pltpu.VMEM((2 * TOK, GROUP * HEAD), BF16), pltpu.VMEM((MAX_TILES, HEAD, TILE_PAD), BF16)]
        + [pltpu.VMEM(kv.shape, BF16)] * 2
        + [pltpu.SemaphoreType.DMA((2, MAX_TILES))] * 2,
        compiler_params=pltpu.CompilerParams(vmem_limit_bytes=60 * 2**20),
    )(place, tiles, starts, ends, owner, qo, go, moved_in, kv)


def shards(queries, out_grad, image_kv, tiles, span_start, span_end, image_owner):
    spans = lax.axis_size("ctx")
    place = lax.axis_index("ctx").astype(jnp.int32).reshape(1)
    earlier = [(i, i - 1) for i in range(1, spans)]
    later = [(i, i + 1) for i in range(spans - 1)]
    moved_in = lax.ppermute(jnp.stack([queries, out_grad]), "ctx", earlier)
    kv = image_kv.reshape(2, MAX_TILES, TILE_ROWS, HEAD)
    kv = jnp.pad(kv, ((0, 0), (0, 0), (0, TILE_PAD - TILE_ROWS), (0, 0)))
    own, other, parts = backward(
        place, tiles, span_start, span_end, image_owner, queries, out_grad, moved_in, kv
    )
    returned = lax.ppermute(other, "ctx", later)
    image = interleave(parts)
    grad_queries = own + returned
    grad_kv = image.reshape(1, MAX_TILES * TILE_ROWS, 2, HEAD).transpose(0, 2, 1, 3)
    return grad_queries, grad_kv


def solution(mesh):
    return jax.shard_map(
        shards,
        mesh=mesh,
        in_specs=(P("ctx", "tp"), P("ctx", "tp"), P("ctx", None, None, "tp"), P(), P(), P(), P()),
        out_specs=(P("ctx", "tp"), P("ctx", None, None, "tp")),
        check_vma=False,
    )
```
